32 devices in a mesh: inst: 4 (over x, core), stream: 4 (over z), rad: 2 (over y).
Axes of the slice: x: 2, y: 2, z: 4, core: 2. Of those that a mesh axis runs over, the one named last changes fastest.
Arguments:
- state: float32 [4, 6, 64, 32, 128], P('inst', None, 'stream', 'rad'), may hold values from -6 to 6
- axial_speed: float32 [64, 32, 128], P('stream', 'rad'), may hold values from 0.5 to 1.5
- cross_speed: float32 [2, 64, 32, 128], P(None, 'stream', 'rad'), may hold values from -0.5 to 0.5
- viscosity: float32 [64, 32, 128], P('stream', 'rad'), may hold values from 0.01 to 0.2
- coupling: float32 [6, 6], replicated, may hold values from -1.5 to 1.5
- targets: int32 [4, 32, 128, 2], P('inst', 'rad'), may hold values from 0 to 511
- shares: float32 [4, 32, 128], P('inst', 'rad'), may hold values from 0.2 to 0.8
Outputs:
- updated: float32 [4, 6, 64, 32, 128], P('inst', None, 'stream', 'rad')
The draws below stay inside these ranges and needn't reach their ends.
Inputs may be any that keep to these rules, and one draw needn't show every extreme that they name: targets[n, r, j, k] = m * 128 + t names slot t of the stator face of instance m.
All inputs are finite; a program needn't handle non-finite values.
Results may differ from the reference program's by a relative error of at most 0.0001.
Values sent between devices are 32-bit elements; how exact they have to be, the bound alone decides.
A program may use at most 64 MiB of HBM per device.

```python
import math
import jax
import jax.numpy as jnp
from jax import lax

V = 6
CT = 128
INSTANCES = 4
NS = 64
NR = 32


def touch_ends(values, stream_key, low, high):
    index_at = [jax.random.randint(jax.random.fold_in(stream_key, axis), (), 0, length) for axis, length in enumerate(values.shape)]
    longest = values.shape.index(max(values.shape))
    neighbour = index_at[:longest] + [(index_at[longest] + 1) % values.shape[longest]] + index_at[longest + 1:]
    return values.at[tuple(index_at)].set(low).at[tuple(neighbour)].set(high)


def levels(key, dims, shards, low, largest):
    loudness, own = 1.0, jax.random.fold_in(key, 6)
    for position, parts in shards:
        steps = jnp.exp(jax.random.uniform(jax.random.fold_in(own, position), (parts,), jnp.float32, low / len(shards), largest / len(shards)))
        loudness = loudness * jnp.repeat(steps, dims[position] // parts).reshape([-1 if axis == position else 1 for axis in range(len(dims))])
    return loudness


def centred(key, dims, spread, reach, cuts=(), kind=jnp.bfloat16):
    loudness = levels(key, dims, cuts, -0.22, 0.18) if cuts else 1.0
    values = jax.random.normal(key, dims, jnp.float32) * spread * loudness
    return jnp.minimum(jnp.maximum(values, -reach), reach).astype(kind)


def setup_inputs(seed: int = 0) -> dict:
    seeds = jax.random.split(jax.random.key(seed), 8)
    return {
        "state": centred(seeds[0], (INSTANCES, V, NS, NR, CT), 1.0, 6.0, ((0, 4), (2, 4), (3, 2)), jnp.float32),
        "axial_speed": jnp.clip(0.5 + 1.0 * jax.random.uniform(seeds[1], (NS, NR, CT), jnp.float32) ** levels(seeds[1], (NS, NR, CT), ((0, 4), (1, 2)), -0.2, 0.2), 0.5, 1.5),
        "cross_speed": jnp.clip(jax.random.uniform(seeds[2], (2, NS, NR, CT), jnp.float32, -0.5, 0.5) * levels(seeds[2], (2, NS, NR, CT), ((1, 4), (2, 2)), -0.4, 0.0), -0.5, 0.5),
        "viscosity": jnp.clip(jnp.exp(math.log(0.2) - 2.9957323 * jax.random.uniform(seeds[3], (NS, NR, CT), jnp.float32) ** levels(seeds[3], (NS, NR, CT), ((0, 4), (1, 2)), -0.2, 0.2)), 0.01, 0.2),
        "coupling": centred(seeds[4], (V, V), 0.3, 1.5, (), jnp.float32),
        "targets": touch_ends(jax.random.randint(seeds[5], (INSTANCES, NR, CT, 2), 0, INSTANCES * CT), jax.random.fold_in(seeds[5], 1), 0, (INSTANCES * CT) - 1).astype(jnp.int32),
        "shares": jnp.clip(0.2 + 0.6 * jax.random.uniform(seeds[6], (INSTANCES, NR, CT), jnp.float32) ** levels(seeds[6], (INSTANCES, NR, CT), ((0, 4), (1, 2)), -0.2, 0.2), 0.2, 0.8),
    }


omega_scale = 0.5
pseudo_step = 0.5


def coefficient(steps, count):
    kf = steps.astype(jnp.float32)
    safe = jnp.where(steps == 0, jnp.ones_like(kf), kf)
    sign = 1.0 - 2.0 * jnp.mod(safe, 2.0)
    angle = jnp.pi * safe / count
    value = omega_scale * 0.5 * sign * jnp.cos(angle) / jnp.sin(angle)
    return jnp.where(steps == 0, jnp.zeros_like(value), value)


def spectral(field):
    count = field.shape[0]
    total = jnp.zeros_like(field)
    for step in range(1, count):
        weight = coefficient(jnp.array(step, jnp.int32), count)
        total = total + weight * jnp.roll(field, step, axis=0)
    return total


def interface(face_flux, targets, shares):
    count, width = face_flux.shape[0], face_flux.shape[3]
    rows = face_flux.shape[2]
    weights = jnp.stack([shares, 1.0 - shares], axis=-1)
    values = face_flux[..., None] * weights[:, None]
    values = jnp.transpose(values, (0, 2, 3, 4, 1))
    row_index = jnp.broadcast_to(jnp.arange(rows, dtype=jnp.int32)[None, :, None, None], targets.shape)
    inflow = jnp.zeros((rows, count * width, face_flux.shape[1]), face_flux.dtype)
    inflow = inflow.at[row_index, targets].add(values)
    inflow = inflow.reshape(rows, count, width, face_flux.shape[1])
    return jnp.transpose(inflow, (1, 3, 0, 2))


def operator(field, axial_speed, cross_speed, viscosity, coupling, targets, shares):
    flux = axial_speed[None, None] * field
    half = field.shape[2] // 2
    up_flux = jnp.concatenate([jnp.zeros_like(flux[:, :, :1]), flux[:, :, :-1]], axis=2)
    inflow = interface(flux[:, :, half - 1], targets, shares)
    up_flux = up_flux.at[:, :, half].set(inflow)
    padded = jnp.pad(field, ((0, 0), (0, 0), (1, 1), (1, 1), (0, 0)))
    s_low = padded[:, :, :-2, 1:-1]
    s_high = padded[:, :, 2:, 1:-1]
    r_low = padded[:, :, 1:-1, :-2]
    r_high = padded[:, :, 1:-1, 2:]
    t_low = jnp.roll(field, 1, axis=4)
    t_high = jnp.roll(field, -1, axis=4)
    radial = cross_speed[0][None, None]
    beside_all = cross_speed[1][None, None]
    advect = jnp.maximum(radial, 0.0) * (field - r_low) + jnp.minimum(radial, 0.0) * (r_high - field)
    advect = advect + jnp.maximum(beside_all, 0.0) * (field - t_low) + jnp.minimum(beside_all, 0.0) * (t_high - field)
    neighbours = s_low + s_high + r_low + r_high + t_low + t_high
    diffuse = viscosity[None, None] * (neighbours - 6.0 * field)
    source = jnp.einsum("vw,nwsrt->nvsrt", coupling, field, precision=lax.Precision.HIGHEST)
    return flux - up_flux + advect - diffuse + source


def reference(state, axial_speed, cross_speed, viscosity, coupling, targets, shares):
    def total(field):
        return spectral(field) + operator(field, axial_speed, cross_speed, viscosity, coupling, targets, shares)

    middle = state - 0.5 * pseudo_step * total(state)
    return state - pseudo_step * total(middle)
```

```python
import functools
import math

import jax
import jax.numpy as jnp
from jax import lax
from jax.experimental import pallas as pl
from jax.experimental.pallas import tpu as pltpu
from jax.sharding import PartitionSpec as P

omega_scale = 0.5
pseudo_step = 0.5
MESH = pl.DeviceIdType.MESH


def coefficients(count):
    once = [0.0] + [
        omega_scale * 0.5 * (-1.0) ** k * math.cos(math.pi * k / count) / math.sin(math.pi * k / count)
        for k in range(1, count)
    ]
    twice = [sum(once[i] * once[(k - i) % count] for i in range(count)) for k in range(count)]
    return once, twice


def chunk_list(planes):
    chunks = [(planes - 1, 1), (0, 1)]
    start = 1
    while start < planes - 1:
        size = min(2, planes - 1 - start)
        chunks.append((start, size))
        start += size
    return chunks


def kernel(
    count, streams, rads, nvars, planes, rows, width,
    u, axial, cross, viscosity, coupling, targets, shares, out,
    up, axp, xb, cb, f, ur, urs, fr, frs, wv, bs, br, ds, dr, gathered,
    local_sem, x_send, x_recv, c_send, c_recv, uz_send, uz_recv, fz_send, fz_recv,
    a_send, a_recv, ur_send, ur_recv, fr_send, fr_recv, b_send, b_recv, d_send, d_recv,
):
    chips = count // 2
    chunks = chunk_list(planes)
    once, twice = coefficients(count)
    half_step = 0.5 * pseudo_step
    vpad = fr.shape[2]
    me = lax.axis_index("inst")
    z = lax.axis_index("stream")
    r = lax.axis_index("rad")
    chip, core = me // 2, lax.rem(me, 2)
    peer = me + 1 - 2 * core
    has_zlo, has_zhi = z > 0, z < streams - 1
    has_rlo, has_rhi = r > 0, r < rads - 1
    face = z == streams // 2 - 1
    stator = z == streams // 2

    def rows_of(s, n=1, shift=0):
        return pl.ds((s + shift) * rows, n * rows)

    def row_at(s, shift=0):
        return pl.ds(pl.multiple_of((s + shift) * rows, rows), rows)

    def x_copy(d, j):
        s, n = chunks[j]
        return pltpu.make_async_remote_copy(
            src_ref=u.at[:, rows_of(s, n), :], dst_ref=xb.at[d - 1, :, rows_of(s, n), :],
            send_sem=x_send.at[d - 1, j], recv_sem=x_recv.at[d - 1, j],
            device_id={"inst": lax.rem(chip + d, chips) * 2 + core}, device_id_type=MESH)

    def c_copy(d, j):
        s, n = chunks[j]
        source = u if d == 0 else xb.at[d - 1]
        return pltpu.make_async_remote_copy(
            src_ref=source.at[:, rows_of(s, n), :], dst_ref=cb.at[d, :, rows_of(s, n), :],
            send_sem=c_send.at[d, j], recv_sem=c_recv.at[d, j],
            device_id={"inst": peer}, device_id_type=MESH)

    def z_copy(to_high, source, shift, field, send, recv):
        own = rows_of(planes - 1 if to_high else 0, 1, shift)
        landing = rows_of(0 if to_high else planes + 1)
        return pltpu.make_async_remote_copy(
            src_ref=source.at[:, own, :], dst_ref=field.at[:, landing, :],
            send_sem=send.at[1 - to_high], recv_sem=recv.at[1 - to_high],
            device_id={"stream": z + 1 if to_high else z - 1}, device_id_type=MESH)

    def uz_copy(to_high):
        return z_copy(to_high, u, 0, up, uz_send, uz_recv)

    def fz_copy(to_high):
        return z_copy(to_high, f, 1, f, fz_send, fz_recv)

    def a_copy():
        return pltpu.make_async_remote_copy(
            src_ref=axial.at[rows_of(planes - 1), :], dst_ref=axp.at[rows_of(0), :],
            send_sem=a_send.at[0], recv_sem=a_recv.at[0],
            device_id={"stream": z + 1}, device_id_type=MESH)

    def ur_copy(to_high):
        side = 1 - to_high
        return pltpu.make_async_remote_copy(
            src_ref=urs.at[side], dst_ref=ur.at[side],
            send_sem=ur_send.at[side], recv_sem=ur_recv.at[side],
            device_id={"rad": r + 1 if to_high else r - 1}, device_id_type=MESH)

    def fr_copy(to_high, j):
        s, n = chunks[j]
        side = 1 - to_high
        return pltpu.make_async_remote_copy(
            src_ref=frs.at[side, pl.ds(s, n)], dst_ref=fr.at[side, pl.ds(s, n)],
            send_sem=fr_send.at[side, j], recv_sem=fr_recv.at[side, j],
            device_id={"rad": r + 1 if to_high else r - 1}, device_id_type=MESH)

    def face_copy(source, landing, send, recv, m, slot):
        return pltpu.make_async_remote_copy(
            src_ref=source.at[m], dst_ref=landing.at[slot],
            send_sem=send.at[m], recv_sem=recv.at[slot],
            device_id={"inst": m, "stream": z + 1}, device_id_type=MESH)

    def local_copies():
        return [
            pltpu.make_async_copy(u, up.at[:, rows_of(0, planes, 1), :], local_sem.at[0]),
            pltpu.make_async_copy(axial, axp.at[rows_of(0, planes, 1), :], local_sem.at[1]),
        ]

    for copy in local_copies():
        copy.start()

    barrier = pltpu.get_barrier_semaphore()

    def greet(**device):
        pl.semaphore_signal(barrier, inc=1, device_id=device, device_id_type=MESH)

    greet(inst=peer)
    for d in range(1, chips):
        greet(inst=lax.rem(chip + d, chips) * 2 + core)
    pl.when(has_zlo)(lambda: greet(stream=z - 1))
    pl.when(has_zhi)(lambda: greet(stream=z + 1))
    pl.when(has_rlo)(lambda: greet(rad=r - 1))
    pl.when(has_rhi)(lambda: greet(rad=r + 1))
    for d in range(1, count):
        other = lax.rem(me + d, count)
        pl.when(face)(functools.partial(greet, inst=other, stream=z + 1))
        pl.when(stator)(functools.partial(greet, inst=other, stream=z - 1))
    one = lambda flag: flag.astype(jnp.int32)
    expected = chips + one(has_zlo) + one(has_zhi) + one(has_rlo) + one(has_rhi)
    expected = expected + (count - 1) * (one(face) + one(stator))

    plane_zero = jnp.zeros((rows, width), jnp.float32)

    def zero_plane(field, p):
        for v in range(nvars):
            field[v, rows_of(p), :] = plane_zero

    @pl.when(jnp.logical_not(has_zlo))
    def _():
        zero_plane(up, 0)
        zero_plane(f, 0)

    @pl.when(jnp.logical_not(has_zhi))
    def _():
        zero_plane(up, planes + 1)
        zero_plane(f, planes + 1)

    no_axial = jnp.logical_or(jnp.logical_not(has_zlo), stator)

    @pl.when(no_axial)
    def _():
        axp[rows_of(0), :] = plane_zero

    @pl.when(jnp.logical_not(has_rlo))
    def _():
        ur[0] = jnp.zeros(ur.shape[1:], jnp.float32)
        fr[0] = jnp.zeros(fr.shape[1:], jnp.float32)

    @pl.when(jnp.logical_not(has_rhi))
    def _():
        ur[1] = jnp.zeros(ur.shape[1:], jnp.float32)
        fr[1] = jnp.zeros(fr.shape[1:], jnp.float32)

    urs[...] = jnp.zeros(urs.shape, jnp.float32)
    frs[...] = jnp.zeros(frs.shape, jnp.float32)
    wv[...] = jnp.zeros(wv.shape, jnp.float32)

    pl.semaphore_wait(barrier, expected)

    for j in range(len(chunks)):
        for d in range(1, chips):
            x_copy(d, j).start()
    for j in range(len(chunks)):
        c_copy(0, j).start()
    pl.when(has_zhi)(lambda: uz_copy(1).start())
    pl.when(has_zlo)(lambda: uz_copy(0).start())
    sends_axial = jnp.logical_and(has_zhi, jnp.logical_not(face))
    pl.when(sends_axial)(lambda: a_copy().start())

    for copy in local_copies():
        copy.wait()

    @pl.loop(0, planes)
    def _(s):
        base = (s + 1) * rows
        for v in range(nvars):
            urs[0, s, v:v + 1, :] = up[v, pl.ds(base + rows - 1, 1), :]
            urs[1, s, v:v + 1, :] = up[v, pl.ds(base, 1), :]

    pl.when(has_rhi)(lambda: ur_copy(1).start())
    pl.when(has_rlo)(lambda: ur_copy(0).start())

    def scatter(result):
        span = min(count, 4) * width

        @pl.loop(0, rows)
        def _(row):
            flux = wv[pl.ds(pl.multiple_of(row * vpad, vpad), vpad), :]
            share = shares[pl.ds(row, 1), :]
            parts = []
            for value in (flux * share, flux * (1.0 - share)):
                high = value.astype(jnp.bfloat16).astype(jnp.float32)
                rest = value - high
                middle = rest.astype(jnp.bfloat16).astype(jnp.float32)
                stack = jnp.concatenate([high, middle, rest - middle], axis=0)
                parts.append(stack.astype(jnp.bfloat16))
            slots = lax.broadcasted_iota(jnp.int32, (span, width), 0)
            for start in range(0, count * width, span):
                total = jnp.zeros((3 * vpad, span), jnp.float32)
                for k in range(2):
                    target = targets[pl.ds(k * rows + row, 1), :]
                    hit = (slots + start == target).astype(jnp.float32).astype(jnp.bfloat16)
                    total = total + lax.dot_general(
                        parts[k], hit, (((1,), (1,)), ((), ())),
                        preferred_element_type=jnp.float32)
                total = total[:vpad] + total[vpad:2 * vpad] + total[2 * vpad:]
                for i in range(span // width):
                    result[start // width + i, pl.ds(pl.multiple_of(row * vpad, vpad), vpad), :] = (
                        total[:, i * width:(i + 1) * width])

    @pl.when(face)
    def _():
        speed = axp[rows_of(planes), :]
        for v in range(nvars):
            wv[pl.ds(v, rows, stride=vpad), :] = speed * up[v, rows_of(planes), :]
        scatter(bs)
        for m in range(count):
            face_copy(bs, br, b_send, b_recv, m, me).start()

    row_index = lax.broadcasted_iota(jnp.int32, (rows, width), 0)
    first_row, last_row = row_index == 0, row_index == rows - 1

    def operator(s, field, halo):
        a = cross[0, row_at(s), :]
        b = cross[1, row_at(s), :]
        nu = viscosity[row_at(s), :]
        ap, am = jnp.maximum(a, 0.0), jnp.minimum(a, 0.0)
        bp, bm = jnp.maximum(b, 0.0), jnp.minimum(b, 0.0)
        centre = axp[row_at(s, 1), :] + (ap - am) + (bp - bm) + 6.0 * nu
        s_low = axp[row_at(s), :] + nu
        r_low, r_high, t_low, t_high = ap + nu, nu - am, bp + nu, nu - bm
        here = [field[v, row_at(s, 1), :] for v in range(nvars)]
        results = []
        for v in range(nvars):
            value = here[v]
            below = jnp.where(first_row, halo[0, s, v:v + 1, :], pltpu.roll(value, 1, 0))
            above = jnp.where(last_row, halo[1, s, v:v + 1, :], pltpu.roll(value, rows - 1, 0))
            total = centre * value
            total = total - s_low * field[v, row_at(s), :] - nu * field[v, row_at(s, 2), :]
            total = total - r_low * below - r_high * above
            total = total - t_low * pltpu.roll(value, 1, 1) - t_high * pltpu.roll(value, width - 1, 1)
            for w in range(nvars):
                total = total + coupling[v, w] * here[w]
            results.append(total)
        return here, results

    pl.when(has_zlo)(lambda: uz_copy(1).wait_recv())
    pl.when(has_zhi)(lambda: uz_copy(0).wait_recv())
    pl.when(jnp.logical_not(no_axial))(lambda: a_copy().wait_recv())
    pl.when(has_rlo)(lambda: ur_copy(1).wait_recv())
    pl.when(has_rhi)(lambda: ur_copy(0).wait_recv())

    @pl.loop(0, planes)
    def _(s):
        here, results = operator(s, up, ur)
        for v in range(nvars):
            f[v, row_at(s, 1), :] = here[v] - half_step * results[v]

    def gather(landing, recv):
        for n in range(count):
            face_copy(landing, landing, recv, recv, 0, n).wait_recv()
        total = landing[0]
        for n in range(1, count):
            total = total + landing[n]
        gathered[...] = total

    @pl.when(stator)
    def _():
        gather(br, b_recv)
        for v in range(nvars):
            f[v, rows_of(0, 1, 1), :] += half_step * gathered[pl.ds(v, rows, stride=vpad), :]

    pairs = [(once[k], once[k] - half_step * twice[k]) for k in range(count)]
    zero_step = lax.convert_element_type(core, jnp.int32) == 0
    terms = []
    for d in range(1, chips):
        terms.append((xb, d - 1, pairs[2 * d]))
    for d in range(chips):
        low, high = pairs[(2 * d - 1) % count], pairs[(2 * d + 1) % count]
        terms.append((cb, d, tuple(jnp.where(zero_step, jnp.float32(lo), jnp.float32(hi)) for lo, hi in zip(low, high))))

    def process(j):
        s0, n = chunks[j]
        for d in range(chips):
            c_copy(d, j).wait_recv()

        for s in range(s0, s0 + n):
            for v in range(nvars):
                own = up[v, rows_of(s, 1, 1), :]
                spectral = pairs[0][0] * own if pairs[0][0] else None
                combined = pairs[0][1] * own
                for buffer, slot, (c, g) in terms:
                    value = buffer[slot, v, rows_of(s), :]
                    spectral = c * value if spectral is None else spectral + c * value
                    combined = combined + g * value
                new = f[v, rows_of(s, 1, 1), :] - pseudo_step * spectral
                f[v, rows_of(s, 1, 1), :] = new
                out[v, rows_of(s), :] = own - pseudo_step * combined
                frs[0, s, v:v + 1, :] = new[rows - 1:rows]
                frs[1, s, v:v + 1, :] = new[0:1]
                if s == planes - 1:
                    wv[pl.ds(v, rows, stride=vpad), :] = axp[rows_of(planes), :] * (new + half_step * spectral)
        pl.when(has_rhi)(lambda: fr_copy(1, j).start())
        pl.when(has_rlo)(lambda: fr_copy(0, j).start())
        if s0 == planes - 1:
            pl.when(has_zhi)(lambda: fz_copy(1).start())

            @pl.when(face)
            def _():
                scatter(ds)
                for m in range(count):
                    total = -ds[m]
                    for k in range(1, count):
                        total = total + (half_step * once[k]) * bs[(m - k) % count]
                    ds[m] = total
                for m in range(count):
                    face_copy(ds, dr, d_send, d_recv, m, me).start()
        if s0 == 0:
            pl.when(has_zlo)(lambda: fz_copy(0).start())

    def finish(s, n):
        @pl.loop(s, s + n)
        def _(s):
            _, results = operator(s, f, fr)
            for v in range(nvars):
                out[v, row_at(s), :] -= pseudo_step * results[v]

    done = {0, planes - 1}
    ready = set()

    def finals(j):
        s0, n = chunks[j]
        pl.when(has_rlo)(lambda: fr_copy(1, j).wait_recv())
        pl.when(has_rhi)(lambda: fr_copy(0, j).wait_recv())
        ready.update(range(s0, s0 + n))
        able = [s for s in range(1, planes - 1)
                if s not in done and {s - 1, s, s + 1} <= ready]
        if able:
            done.update(able)
            finish(able[0], len(able))
        if j == len(chunks) - 2:
            pl.when(has_zlo)(lambda: fz_copy(1).wait_recv())
            pl.when(has_zhi)(lambda: fz_copy(0).wait_recv())
            finish(0, 1)

            @pl.when(stator)
            def _():
                gather(dr, d_recv)
                for v in range(nvars):
                    out[v, rows_of(0), :] -= pseudo_step * gathered[pl.ds(v, rows, stride=vpad), :]
        if j == len(chunks) - 1:
            finish(planes - 1, 1)

    steps = len(chunks)
    for j in range(steps + 2):
        if j < steps:
            for d in range(1, chips):
                x_copy(d, j).wait_recv()
                c_copy(d, j).start()
        if 1 <= j <= steps:
            process(j - 1)
        if 2 <= j:
            finals(j - 2)

    for j in range(steps):
        for d in range(1, chips):
            x_copy(d, j).wait_send()
        for d in range(chips):
            c_copy(d, j).wait_send()
    @pl.when(has_rhi)
    def _():
        ur_copy(1).wait_send()
        for j in range(steps):
            fr_copy(1, j).wait_send()

    @pl.when(has_rlo)
    def _():
        ur_copy(0).wait_send()
        for j in range(steps):
            fr_copy(0, j).wait_send()

    @pl.when(has_zhi)
    def _():
        uz_copy(1).wait_send()
        fz_copy(1).wait_send()

    @pl.when(has_zlo)
    def _():
        uz_copy(0).wait_send()
        fz_copy(0).wait_send()

    pl.when(sends_axial)(lambda: a_copy().wait_send())

    @pl.when(face)
    def _():
        for m in range(count):
            face_copy(bs, br, b_send, b_recv, m, me).wait_send()
            face_copy(ds, dr, d_send, d_recv, m, me).wait_send()


def body(state, axial_speed, cross_speed, viscosity, coupling, targets, shares):
    count, streams, rads = (lax.axis_size(name) for name in ("inst", "stream", "rad"))
    _, nvars, planes, rows, width = state.shape
    chips, chunks = count // 2, len(chunk_list(planes))
    vpad = -(-nvars // 8) * 8
    cells = planes * rows
    vmem = pl.BlockSpec(memory_space=pltpu.VMEM)
    dma = pltpu.SemaphoreType.DMA
    buf = lambda *shape: pltpu.VMEM(shape, jnp.float32)
    result = pl.pallas_call(
        functools.partial(kernel, count, streams, rads, nvars, planes, rows, width),
        out_shape=jax.ShapeDtypeStruct((nvars, cells, width), jnp.float32),
        in_specs=[pl.BlockSpec(memory_space=pl.ANY), vmem, vmem, vmem,
                  pl.BlockSpec(memory_space=pltpu.SMEM), vmem, vmem],
        out_specs=vmem,
        scratch_shapes=[
            buf(nvars, cells + 2 * rows, width), buf(cells + rows, width),
            buf(chips - 1, nvars, cells, width), buf(chips, nvars, cells, width),
            buf(nvars, cells + 2 * rows, width),
            buf(2, planes, vpad, width), buf(2, planes, vpad, width),
            buf(2, planes, vpad, width), buf(2, planes, vpad, width),
            buf(rows * vpad, width),
            buf(count, rows * vpad, width), buf(count, rows * vpad, width),
            buf(count, rows * vpad, width), buf(count, rows * vpad, width),
            buf(rows * vpad, width),
            dma((2,)), dma((chips - 1, chunks)), dma((chips - 1, chunks)),
            dma((chips, chunks)), dma((chips, chunks)),
            dma((2,)), dma((2,)), dma((2,)), dma((2,)), dma((1,)), dma((1,)),
            dma((2,)), dma((2,)), dma((2, chunks)), dma((2, chunks)),
            dma((count,)), dma((count,)), dma((count,)), dma((count,)),
        ],
        compiler_params=pltpu.CompilerParams(
            collective_id=0, has_side_effects=True, vmem_limit_bytes=48 * 1024 * 1024),
    )(
        state.reshape(nvars, cells, width), axial_speed.reshape(cells, width),
        cross_speed.reshape(2, cells, width), viscosity.reshape(cells, width), coupling,
        jnp.transpose(targets[0], (2, 0, 1)).reshape(2 * rows, width), shares[0],
    )
    return result.reshape(state.shape)


def solution(mesh):
    in_specs = (
        P("inst", None, "stream", "rad", None),
        P("stream", "rad", None),
        P(None, "stream", "rad", None),
        P("stream", "rad", None),
        P(),
        P("inst", "rad", None, None),
        P("inst", "rad", None),
    )
    out_specs = P("inst", None, "stream", "rad", None)
    return jax.shard_map(body, mesh=mesh, in_specs=in_specs, out_specs=out_specs, check_vma=False)
```

```python
import functools
import math

import jax
import jax.numpy as jnp
from jax import lax
from jax.experimental import pallas as pl
from jax.experimental.pallas import tpu as pltpu
from jax.sharding import PartitionSpec as P

omega_scale = 0.5
pseudo_step = 0.5
MESH = pl.DeviceIdType.MESH


def coefficients(count):
    once = [0.0] + [
        omega_scale * 0.5 * (-1.0) ** k * math.cos(math.pi * k / count) / math.sin(math.pi * k / count)
        for k in range(1, count)
    ]
    twice = [sum(once[i] * once[(k - i) % count] for i in range(count)) for k in range(count)]
    return once, twice


def chunk_list(planes):
    chunks = [(planes - 1, 1)]
    start = 1
    while start < planes - 1:
        size = min(2, planes - 1 - start)
        chunks.append((start, size))
        start += size
    chunks.insert(len(chunks) - 2, (0, 1))
    return chunks


def kernel(
    count, streams, rads, nvars, planes, rows, width,
    u, axial, cross_in, viscosity_in, coupling, targets_in, shares_in, out,
    up, axp, cross, viscosity, targets, shares, wide, xb, cb, f, ur, urs, fr, frs, wv, bs, br, ds, dr,
    local_sem, x_send, x_recv, c_send, c_recv, uz_send, uz_recv, fz_send, fz_recv,
    a_send, a_recv, ur_send, ur_recv, fr_send, fr_recv, b_send, b_recv, d_send, d_recv,
):
    chips = count // 2
    chunks = chunk_list(planes)
    once, twice = coefficients(count)
    half_step = 0.5 * pseudo_step
    vpad = fr.shape[2]
    me = lax.axis_index("inst")
    z = lax.axis_index("stream")
    r = lax.axis_index("rad")
    chip, core = me // 2, lax.rem(me, 2)
    peer = me + 1 - 2 * core
    has_zlo, has_zhi = z > 0, z < streams - 1
    has_rlo, has_rhi = r > 0, r < rads - 1
    face = z == streams // 2 - 1
    stator = z == streams // 2

    def rows_of(s, n=1, shift=0):
        return pl.ds((s + shift) * rows, n * rows)

    def row_at(s, shift=0):
        return pl.ds(pl.multiple_of((s + shift) * rows, rows), rows)

    def x_copy(d, j):
        s, n = chunks[j]
        return pltpu.make_async_remote_copy(
            src_ref=u.at[:, rows_of(s, n), :], dst_ref=xb.at[d - 1, :, rows_of(s, n), :],
            send_sem=x_send.at[d - 1, j], recv_sem=x_recv.at[d - 1, j],
            device_id={"inst": lax.rem(chip + d, chips) * 2 + core}, device_id_type=MESH)

    def c_copy(d, j):
        s, n = chunks[j]
        source = u if d == 0 else xb.at[d - 1]
        return pltpu.make_async_remote_copy(
            src_ref=source.at[:, rows_of(s, n), :], dst_ref=cb.at[d, :, rows_of(s, n), :],
            send_sem=c_send.at[d, j], recv_sem=c_recv.at[d, j],
            device_id={"inst": peer}, device_id_type=MESH)

    def z_copy(to_high, source, shift, field, send, recv):
        own = rows_of(planes - 1 if to_high else 0, 1, shift)
        landing = rows_of(0 if to_high else planes + 1)
        return pltpu.make_async_remote_copy(
            src_ref=source.at[:, own, :], dst_ref=field.at[:, landing, :],
            send_sem=send.at[1 - to_high], recv_sem=recv.at[1 - to_high],
            device_id={"stream": z + 1 if to_high else z - 1}, device_id_type=MESH)

    def uz_copy(to_high):
        return z_copy(to_high, u, 0, up, uz_send, uz_recv)

    def fz_copy(to_high):
        return z_copy(to_high, f, 1, f, fz_send, fz_recv)

    def a_copy():
        return pltpu.make_async_remote_copy(
            src_ref=axial.at[rows_of(planes - 1), :], dst_ref=axp.at[rows_of(0), :],
            send_sem=a_send.at[0], recv_sem=a_recv.at[0],
            device_id={"stream": z + 1}, device_id_type=MESH)

    def ur_copy(to_high):
        side = 1 - to_high
        return pltpu.make_async_remote_copy(
            src_ref=urs.at[side], dst_ref=ur.at[side],
            send_sem=ur_send.at[side], recv_sem=ur_recv.at[side],
            device_id={"rad": r + 1 if to_high else r - 1}, device_id_type=MESH)

    def fr_copy(to_high, j):
        s, n = chunks[j]
        side = 1 - to_high
        return pltpu.make_async_remote_copy(
            src_ref=frs.at[side, pl.ds(s, n)], dst_ref=fr.at[side, pl.ds(s, n)],
            send_sem=fr_send.at[side, j], recv_sem=fr_recv.at[side, j],
            device_id={"rad": r + 1 if to_high else r - 1}, device_id_type=MESH)

    def face_copy(source, landing, send, recv, m, slot):
        return pltpu.make_async_remote_copy(
            src_ref=source.at[m], dst_ref=landing.at[slot],
            send_sem=send.at[m], recv_sem=recv.at[slot],
            device_id={"inst": m, "stream": z + 1}, device_id_type=MESH)

    def local_copies(first=0, last=6):
        pairs = [
            (u, up.at[:, rows_of(0, planes, 1), :]),
            (axial, axp.at[rows_of(0, planes, 1), :]),
            (targets_in, targets),
            (shares_in, shares),
            (viscosity_in, viscosity),
            (cross_in, cross),
        ]
        return [pltpu.make_async_copy(*pairs[i], local_sem.at[i]) for i in range(first, last)]

    for copy in local_copies():
        copy.start()

    barrier = pltpu.get_barrier_semaphore()

    def greet(**device):
        pl.semaphore_signal(barrier, inc=1, device_id=device, device_id_type=MESH)

    greet(inst=peer)
    for d in range(1, chips):
        greet(inst=lax.rem(chip + d, chips) * 2 + core)
    pl.when(has_zlo)(lambda: greet(stream=z - 1))
    pl.when(has_zhi)(lambda: greet(stream=z + 1))
    pl.when(has_rlo)(lambda: greet(rad=r - 1))
    pl.when(has_rhi)(lambda: greet(rad=r + 1))
    for d in range(1, count):
        other = lax.rem(me + d, count)
        pl.when(face)(functools.partial(greet, inst=other, stream=z + 1))
        pl.when(stator)(functools.partial(greet, inst=other, stream=z - 1))
    one = lambda flag: flag.astype(jnp.int32)
    expected = chips + one(has_zlo) + one(has_zhi) + one(has_rlo) + one(has_rhi)
    expected = expected + (count - 1) * (one(face) + one(stator))

    plane_zero = jnp.zeros((rows, width), jnp.float32)

    def zero_plane(field, p):
        for v in range(nvars):
            field[v, rows_of(p), :] = plane_zero

    @pl.when(jnp.logical_not(has_zlo))
    def _():
        zero_plane(up, 0)
        zero_plane(f, 0)

    @pl.when(jnp.logical_not(has_zhi))
    def _():
        zero_plane(up, planes + 1)
        zero_plane(f, planes + 1)

    no_axial = jnp.logical_or(jnp.logical_not(has_zlo), stator)

    @pl.when(no_axial)
    def _():
        axp[rows_of(0), :] = plane_zero

    @pl.when(jnp.logical_not(has_rlo))
    def _():
        ur[0] = jnp.zeros(ur.shape[1:], jnp.float32)
        fr[0] = jnp.zeros(fr.shape[1:], jnp.float32)

    @pl.when(jnp.logical_not(has_rhi))
    def _():
        ur[1] = jnp.zeros(ur.shape[1:], jnp.float32)
        fr[1] = jnp.zeros(fr.shape[1:], jnp.float32)

    urs[...] = jnp.zeros(urs.shape, jnp.float32)
    frs[...] = jnp.zeros(frs.shape, jnp.float32)
    wv[...] = jnp.zeros(wv.shape, jnp.float32)

    pl.semaphore_wait(barrier, expected)

    early = min(5, len(chunks))
    for j in range(early):
        for d in range(1, chips):
            x_copy(d, j).start()
    for j in range(len(chunks)):
        c_copy(0, j).start()
    pl.when(has_zhi)(lambda: uz_copy(1).start())
    pl.when(has_zlo)(lambda: uz_copy(0).start())
    sends_axial = jnp.logical_and(has_zhi, jnp.logical_not(face))
    pl.when(sends_axial)(lambda: a_copy().start())

    for copy in local_copies(0, 4):
        copy.wait()

    @pl.loop(0, planes)
    def _(s):
        base = (s + 1) * rows
        for v in range(nvars):
            urs[0, s, v:v + 1, :] = up[v, pl.ds(base + rows - 1, 1), :]
            urs[1, s, v:v + 1, :] = up[v, pl.ds(base, 1), :]

    pl.when(has_rhi)(lambda: ur_copy(1).start())
    pl.when(has_rlo)(lambda: ur_copy(0).start())

    def scatter(result):
        span = min(count, 4) * width

        @pl.loop(0, rows)
        def _(row):
            flux = wv[pl.ds(pl.multiple_of(row * vpad, vpad), vpad), :]
            share = shares[pl.ds(row, 1), :]
            parts = []
            for value in (flux * share, flux * (1.0 - share)):
                high = value.astype(jnp.bfloat16).astype(jnp.float32)
                rest = value - high
                middle = rest.astype(jnp.bfloat16).astype(jnp.float32)
                stack = jnp.concatenate([high, middle, rest - middle], axis=0)
                parts.append(stack.astype(jnp.bfloat16))
            slots = lax.broadcasted_iota(jnp.int32, (span, width), 0)
            for start in range(0, count * width, span):
                total = jnp.zeros((3 * vpad, span), jnp.float32)
                for k in range(2):
                    target = targets[pl.ds(k * rows + row, 1), :]
                    hit = (slots + start == target).astype(jnp.float32).astype(jnp.bfloat16)
                    total = total + lax.dot_general(
                        parts[k], hit, (((1,), (1,)), ((), ())),
                        preferred_element_type=jnp.float32)
                total = total[:vpad] + total[vpad:2 * vpad] + total[2 * vpad:]
                for i in range(span // width):
                    wide[start // width + i, pl.ds(pl.multiple_of(row * vpad, vpad), vpad), :] = (
                        total[:, i * width:(i + 1) * width])

        for m in range(count):
            for v in range(nvars):
                result[m, v] = wide[m, pl.ds(v, rows, stride=vpad), :]

    @pl.when(face)
    def _():
        speed = axp[rows_of(planes), :]
        for v in range(nvars):
            wv[pl.ds(v, rows, stride=vpad), :] = speed * up[v, rows_of(planes), :]
        scatter(bs)
        for m in range(count):
            face_copy(bs, br, b_send, b_recv, m, me).start()

    row_index = lax.broadcasted_iota(jnp.int32, (rows, width), 0)
    first_row, last_row = row_index == 0, row_index == rows - 1

    def operator(s, field, halo):
        a = cross[0, row_at(s), :]
        b = cross[1, row_at(s), :]
        nu = viscosity[row_at(s), :]
        ap, am = jnp.maximum(a, 0.0), jnp.minimum(a, 0.0)
        bp, bm = jnp.maximum(b, 0.0), jnp.minimum(b, 0.0)
        centre = axp[row_at(s, 1), :] + (ap - am) + (bp - bm) + 6.0 * nu
        s_low = axp[row_at(s), :] + nu
        r_low, r_high, t_low, t_high = ap + nu, nu - am, bp + nu, nu - bm
        here = [field[v, row_at(s, 1), :] for v in range(nvars)]
        results = []
        for v in range(nvars):
            value = here[v]
            below = jnp.where(first_row, halo[0, s, v:v + 1, :], pltpu.roll(value, 1, 0))
            above = jnp.where(last_row, halo[1, s, v:v + 1, :], pltpu.roll(value, rows - 1, 0))
            total = centre * value
            total = total - s_low * field[v, row_at(s), :] - nu * field[v, row_at(s, 2), :]
            total = total - r_low * below - r_high * above
            total = total - t_low * pltpu.roll(value, 1, 1) - t_high * pltpu.roll(value, width - 1, 1)
            for w in range(nvars):
                total = total + coupling[v, w] * here[w]
            results.append(total)
        return here, results

    for copy in local_copies(4):
        copy.wait()
    pl.when(has_zlo)(lambda: uz_copy(1).wait_recv())
    pl.when(has_zhi)(lambda: uz_copy(0).wait_recv())
    pl.when(jnp.logical_not(no_axial))(lambda: a_copy().wait_recv())
    pl.when(has_rlo)(lambda: ur_copy(1).wait_recv())
    pl.when(has_rhi)(lambda: ur_copy(0).wait_recv())

    @pl.loop(0, planes)
    def _(s):
        here, results = operator(s, up, ur)
        for v in range(nvars):
            f[v, row_at(s, 1), :] = here[v] - half_step * results[v]

    def gather(landing, recv):
        for n in range(count):
            face_copy(landing, landing, recv, recv, 0, n).wait_recv()
        return [sum((landing[n, v] for n in range(1, count)), landing[0, v]) for v in range(nvars)]

    pairs = [(once[k], once[k] - half_step * twice[k]) for k in range(count)]
    zero_step = lax.convert_element_type(core, jnp.int32) == 0
    terms = []
    for d in range(1, chips):
        terms.append((xb, d - 1, pairs[2 * d]))
    for d in range(chips):
        low, high = pairs[(2 * d - 1) % count], pairs[(2 * d + 1) % count]
        terms.append((cb, d, tuple(jnp.where(zero_step, jnp.float32(lo), jnp.float32(hi)) for lo, hi in zip(low, high))))

    def process(j):
        s0, n = chunks[j]
        for d in range(chips):
            c_copy(d, j).wait_recv()
        if s0 == 0:
            @pl.when(stator)
            def _():
                for v, inflow in enumerate(gather(br, b_recv)):
                    f[v, rows_of(0, 1, 1), :] += half_step * inflow

        for s in range(s0, s0 + n):
            for v in range(nvars):
                own = up[v, rows_of(s, 1, 1), :]
                spectral = pairs[0][0] * own if pairs[0][0] else None
                combined = pairs[0][1] * own
                for buffer, slot, (c, g) in terms:
                    value = buffer[slot, v, rows_of(s), :]
                    spectral = c * value if spectral is None else spectral + c * value
                    combined = combined + g * value
                new = f[v, rows_of(s, 1, 1), :] - pseudo_step * spectral
                f[v, rows_of(s, 1, 1), :] = new
                out[v, rows_of(s), :] = own - pseudo_step * combined
                frs[0, s, v:v + 1, :] = new[rows - 1:rows]
                frs[1, s, v:v + 1, :] = new[0:1]
                if s == planes - 1:
                    wv[pl.ds(v, rows, stride=vpad), :] = axp[rows_of(planes), :] * (new + half_step * spectral)
        pl.when(has_rhi)(lambda: fr_copy(1, j).start())
        pl.when(has_rlo)(lambda: fr_copy(0, j).start())
        if s0 == planes - 1:
            pl.when(has_zhi)(lambda: fz_copy(1).start())

            @pl.when(face)
            def _():
                scatter(ds)
                for m in range(count):
                    total = -ds[m]
                    for k in range(1, count):
                        total = total + (half_step * once[k]) * bs[(m - k) % count]
                    ds[m] = total
                for m in range(count):
                    face_copy(ds, dr, d_send, d_recv, m, me).start()
        if s0 == 0:
            pl.when(has_zlo)(lambda: fz_copy(0).start())

    def finish(s, n):
        @pl.loop(s, s + n)
        def _(s):
            _, results = operator(s, f, fr)
            for v in range(nvars):
                out[v, row_at(s), :] -= pseudo_step * results[v]

    done = {0, planes - 1}
    ready = set()

    def finals(j):
        s0, n = chunks[j]
        pl.when(has_rlo)(lambda: fr_copy(1, j).wait_recv())
        pl.when(has_rhi)(lambda: fr_copy(0, j).wait_recv())
        ready.update(range(s0, s0 + n))
        able = [s for s in range(1, planes - 1)
                if s not in done and {s - 1, s, s + 1} <= ready]
        if able:
            done.update(able)
            finish(able[0], len(able))
        if j == len(chunks) - 2:
            pl.when(has_zlo)(lambda: fz_copy(1).wait_recv())
            finish(0, 1)
        if j == len(chunks) - 1:
            pl.when(has_zhi)(lambda: fz_copy(0).wait_recv())
            finish(planes - 1, 1)

            @pl.when(stator)
            def _():
                for v, inflow in enumerate(gather(dr, d_recv)):
                    out[v, rows_of(0), :] -= pseudo_step * inflow

    steps = len(chunks)
    for j in range(steps + 2):
        if j < steps:
            for d in range(1, chips):
                x_copy(d, j).wait_recv()
                c_copy(d, j).start()
        if 1 <= j <= steps:
            process(j - 1)
        if j == 1:
            for later in range(early, steps):
                for d in range(1, chips):
                    x_copy(d, later).start()
        if 2 <= j:
            finals(j - 2)

    for j in range(steps):
        for d in range(1, chips):
            x_copy(d, j).wait_send()
        for d in range(chips):
            c_copy(d, j).wait_send()
    @pl.when(has_rhi)
    def _():
        ur_copy(1).wait_send()
        for j in range(steps):
            fr_copy(1, j).wait_send()

    @pl.when(has_rlo)
    def _():
        ur_copy(0).wait_send()
        for j in range(steps):
            fr_copy(0, j).wait_send()

    @pl.when(has_zhi)
    def _():
        uz_copy(1).wait_send()
        fz_copy(1).wait_send()

    @pl.when(has_zlo)
    def _():
        uz_copy(0).wait_send()
        fz_copy(0).wait_send()

    pl.when(sends_axial)(lambda: a_copy().wait_send())

    @pl.when(face)
    def _():
        for m in range(count):
            face_copy(bs, br, b_send, b_recv, m, me).wait_send()
            face_copy(ds, dr, d_send, d_recv, m, me).wait_send()


def body(state, axial_speed, cross_speed, viscosity, coupling, targets, shares):
    count, streams, rads = (lax.axis_size(name) for name in ("inst", "stream", "rad"))
    _, nvars, planes, rows, width = state.shape
    chips, chunks = count // 2, len(chunk_list(planes))
    vpad = -(-nvars // 8) * 8
    cells = planes * rows
    vmem = pl.BlockSpec(memory_space=pltpu.VMEM)
    hbm = pl.BlockSpec(memory_space=pltpu.HBM)
    dma = pltpu.SemaphoreType.DMA
    buf = lambda *shape: pltpu.VMEM(shape, jnp.float32)
    result = pl.pallas_call(
        functools.partial(kernel, count, streams, rads, nvars, planes, rows, width),
        out_shape=jax.ShapeDtypeStruct((nvars, cells, width), jnp.float32),
        in_specs=[hbm, hbm, hbm, hbm, pl.BlockSpec(memory_space=pltpu.SMEM), hbm, hbm],
        out_specs=vmem,
        scratch_shapes=[
            buf(nvars, cells + 2 * rows, width), buf(cells + rows, width),
            buf(2, cells, width), buf(cells, width),
            pltpu.VMEM((2 * rows, width), jnp.int32), buf(rows, width),
            buf(count, rows * vpad, width),
            buf(chips - 1, nvars, cells, width), buf(chips, nvars, cells, width),
            buf(nvars, cells + 2 * rows, width),
            buf(2, planes, vpad, width), buf(2, planes, vpad, width),
            buf(2, planes, vpad, width), buf(2, planes, vpad, width),
            buf(rows * vpad, width),
            buf(count, nvars, rows, width), buf(count, nvars, rows, width),
            buf(count, nvars, rows, width), buf(count, nvars, rows, width),
            dma((6,)), dma((chips - 1, chunks)), dma((chips - 1, chunks)),
            dma((chips, chunks)), dma((chips, chunks)),
            dma((2,)), dma((2,)), dma((2,)), dma((2,)), dma((1,)), dma((1,)),
            dma((2,)), dma((2,)), dma((2, chunks)), dma((2, chunks)),
            dma((count,)), dma((count,)), dma((count,)), dma((count,)),
        ],
        compiler_params=pltpu.CompilerParams(
            collective_id=0, has_side_effects=True, vmem_limit_bytes=63 * 1024 * 1024),
    )(
        state.reshape(nvars, cells, width), axial_speed.reshape(cells, width),
        cross_speed.reshape(2, cells, width), viscosity.reshape(cells, width), coupling,
        jnp.transpose(targets[0], (2, 0, 1)).reshape(2 * rows, width), shares[0],
    )
    return result.reshape(state.shape)


def solution(mesh):
    in_specs = (
        P("inst", None, "stream", "rad", None),
        P("stream", "rad", None),
        P(None, "stream", "rad", None),
        P("stream", "rad", None),
        P(),
        P("inst", "rad", None, None),
        P("inst", "rad", None),
    )
    out_specs = P("inst", None, "stream", "rad", None)
    return jax.shard_map(body, mesh=mesh, in_specs=in_specs, out_specs=out_specs, check_vma=False)
```

```python
import functools
import math

import jax
import jax.numpy as jnp
from jax import lax
from jax.experimental import pallas as pl
from jax.experimental.pallas import tpu as pltpu
from jax.sharding import PartitionSpec as P

omega_scale = 0.5
pseudo_step = 0.5
MESH = pl.DeviceIdType.MESH


def coefficients(count):
    once = [0.0] + [
        omega_scale * 0.5 * (-1.0) ** k * math.cos(math.pi * k / count) / math.sin(math.pi * k / count)
        for k in range(1, count)
    ]
    twice = [sum(once[i] * once[(k - i) % count] for i in range(count)) for k in range(count)]
    return once, twice


def chunk_list(planes):
    chunks = [(planes - 1, 1)]
    start = 1
    while start < planes - 1:
        size = min(2, planes - 1 - start)
        chunks.append((start, size))
        start += size
    chunks.insert(len(chunks) - 2, (0, 1))
    return chunks


def kernel(
    count, streams, rads, nvars, planes, rows, width,
    u, axial, cross_in, viscosity_in, coupling, targets_in, shares_in, out,
    up, axp, cross, viscosity, targets, shares, wide, xb, cb, f, ur, urs, fr, frs, wv, bs, br,
    local_sem, x_send, x_recv, c_send, c_recv, uz_send, uz_recv, fz_send, fz_recv,
    a_send, a_recv, ur_send, ur_recv, fr_send, fr_recv, b_send, b_recv,
):
    chips = count // 2
    chunks = chunk_list(planes)
    once, twice = coefficients(count)
    half_step = 0.5 * pseudo_step
    vpad = fr.shape[2]
    me = lax.axis_index("inst")
    z = lax.axis_index("stream")
    r = lax.axis_index("rad")
    chip, core = me // 2, lax.rem(me, 2)
    peer = me + 1 - 2 * core
    has_zlo, has_zhi = z > 0, z < streams - 1
    has_rlo, has_rhi = r > 0, r < rads - 1
    face = z == streams // 2 - 1
    stator = z == streams // 2

    def rows_of(s, n=1, shift=0):
        return pl.ds((s + shift) * rows, n * rows)

    def row_at(s, shift=0):
        return pl.ds(pl.multiple_of((s + shift) * rows, rows), rows)

    def x_copy(d, j):
        s, n = chunks[j]
        return pltpu.make_async_remote_copy(
            src_ref=u.at[:, rows_of(s, n), :], dst_ref=xb.at[d - 1, :, rows_of(s, n), :],
            send_sem=x_send.at[d - 1, j], recv_sem=x_recv.at[d - 1, j],
            device_id={"inst": lax.rem(chip + d, chips) * 2 + core}, device_id_type=MESH)

    def c_copy(d, j):
        s, n = chunks[j]
        source = u if d == 0 else xb.at[d - 1]
        return pltpu.make_async_remote_copy(
            src_ref=source.at[:, rows_of(s, n), :], dst_ref=cb.at[d, :, rows_of(s, n), :],
            send_sem=c_send.at[d, j], recv_sem=c_recv.at[d, j],
            device_id={"inst": peer}, device_id_type=MESH)

    def z_copy(to_high, source, shift, field, send, recv):
        own = rows_of(planes - 1 if to_high else 0, 1, shift)
        landing = rows_of(0 if to_high else planes + 1)
        return pltpu.make_async_remote_copy(
            src_ref=source.at[:, own, :], dst_ref=field.at[:, landing, :],
            send_sem=send.at[1 - to_high], recv_sem=recv.at[1 - to_high],
            device_id={"stream": z + 1 if to_high else z - 1}, device_id_type=MESH)

    def uz_copy(to_high):
        return z_copy(to_high, u, 0, up, uz_send, uz_recv)

    def fz_copy(to_high):
        return z_copy(to_high, f, 1, f, fz_send, fz_recv)

    def a_copy():
        return pltpu.make_async_remote_copy(
            src_ref=axial.at[rows_of(planes - 1), :], dst_ref=axp.at[rows_of(0), :],
            send_sem=a_send.at[0], recv_sem=a_recv.at[0],
            device_id={"stream": z + 1}, device_id_type=MESH)

    def ur_copy(to_high):
        side = 1 - to_high
        return pltpu.make_async_remote_copy(
            src_ref=urs.at[side], dst_ref=ur.at[side],
            send_sem=ur_send.at[side], recv_sem=ur_recv.at[side],
            device_id={"rad": r + 1 if to_high else r - 1}, device_id_type=MESH)

    def fr_copy(to_high, j):
        s, n = chunks[j]
        side = 1 - to_high
        return pltpu.make_async_remote_copy(
            src_ref=frs.at[side, pl.ds(s, n)], dst_ref=fr.at[side, pl.ds(s, n)],
            send_sem=fr_send.at[side, j], recv_sem=fr_recv.at[side, j],
            device_id={"rad": r + 1 if to_high else r - 1}, device_id_type=MESH)

    def face_copy(m, slot):
        return pltpu.make_async_remote_copy(
            src_ref=bs.at[m], dst_ref=br.at[slot],
            send_sem=b_send.at[m], recv_sem=b_recv.at[slot],
            device_id={"inst": m, "stream": z + 1}, device_id_type=MESH)

    def local_copies(first=0, last=6):
        pairs = [
            (u, up.at[:, rows_of(0, planes, 1), :]),
            (axial, axp.at[rows_of(0, planes, 1), :]),
            (targets_in, targets),
            (shares_in, shares),
            (viscosity_in, viscosity),
            (cross_in, cross),
        ]
        return [pltpu.make_async_copy(*pairs[i], local_sem.at[i]) for i in range(first, last)]

    for copy in local_copies():
        copy.start()

    barrier = pltpu.get_barrier_semaphore()

    def greet(**device):
        pl.semaphore_signal(barrier, inc=1, device_id=device, device_id_type=MESH)

    greet(inst=peer)
    for d in range(1, chips):
        greet(inst=lax.rem(chip + d, chips) * 2 + core)
    pl.when(has_zlo)(lambda: greet(stream=z - 1))
    pl.when(has_zhi)(lambda: greet(stream=z + 1))
    pl.when(has_rlo)(lambda: greet(rad=r - 1))
    pl.when(has_rhi)(lambda: greet(rad=r + 1))
    for d in range(1, count):
        other = lax.rem(me + d, count)
        pl.when(face)(functools.partial(greet, inst=other, stream=z + 1))
        pl.when(stator)(functools.partial(greet, inst=other, stream=z - 1))
    one = lambda flag: flag.astype(jnp.int32)
    expected = chips + one(has_zlo) + one(has_zhi) + one(has_rlo) + one(has_rhi)
    expected = expected + (count - 1) * (one(face) + one(stator))

    plane_zero = jnp.zeros((rows, width), jnp.float32)

    def zero_plane(field, p):
        for v in range(nvars):
            field[v, rows_of(p), :] = plane_zero

    @pl.when(jnp.logical_not(has_zlo))
    def _():
        zero_plane(up, 0)
        zero_plane(f, 0)

    @pl.when(jnp.logical_not(has_zhi))
    def _():
        zero_plane(up, planes + 1)
        zero_plane(f, planes + 1)

    no_axial = jnp.logical_or(jnp.logical_not(has_zlo), stator)

    @pl.when(no_axial)
    def _():
        axp[rows_of(0), :] = plane_zero

    @pl.when(jnp.logical_not(has_rlo))
    def _():
        ur[0] = jnp.zeros(ur.shape[1:], jnp.float32)
        fr[0] = jnp.zeros(fr.shape[1:], jnp.float32)

    @pl.when(jnp.logical_not(has_rhi))
    def _():
        ur[1] = jnp.zeros(ur.shape[1:], jnp.float32)
        fr[1] = jnp.zeros(fr.shape[1:], jnp.float32)

    urs[...] = jnp.zeros(urs.shape, jnp.float32)
    frs[...] = jnp.zeros(frs.shape, jnp.float32)
    wv[...] = jnp.zeros(wv.shape, jnp.float32)

    pl.semaphore_wait(barrier, expected)

    early = min(5, len(chunks))
    for j in range(early):
        for d in range(1, chips):
            x_copy(d, j).start()
    for j in range(len(chunks)):
        c_copy(0, j).start()
    pl.when(has_zhi)(lambda: uz_copy(1).start())
    pl.when(has_zlo)(lambda: uz_copy(0).start())
    sends_axial = jnp.logical_and(has_zhi, jnp.logical_not(face))
    pl.when(sends_axial)(lambda: a_copy().start())

    for copy in local_copies(0, 4):
        copy.wait()

    @pl.loop(0, planes)
    def _(s):
        base = (s + 1) * rows
        for v in range(nvars):
            urs[0, s, v:v + 1, :] = up[v, pl.ds(base + rows - 1, 1), :]
            urs[1, s, v:v + 1, :] = up[v, pl.ds(base, 1), :]

    pl.when(has_rhi)(lambda: ur_copy(1).start())
    pl.when(has_rlo)(lambda: ur_copy(0).start())

    fpad = wv.shape[0] // rows

    def scatter():
        span = min(count, 4) * width

        def one_row(row, _):
            flux = wv[pl.ds(pl.multiple_of(row * fpad, fpad), fpad), :]
            share = shares[pl.ds(row, 1), :]
            parts = []
            for value in (flux * share, flux * (1.0 - share)):
                high = value.astype(jnp.bfloat16).astype(jnp.float32)
                rest = value - high
                middle = rest.astype(jnp.bfloat16).astype(jnp.float32)
                stack = jnp.concatenate([high, middle, rest - middle], axis=0)
                parts.append(stack.astype(jnp.bfloat16))
            left = jnp.concatenate(parts, axis=1)
            slots = lax.broadcasted_iota(jnp.int32, (span, width), 0)
            for start in range(0, count * width, span):
                hits = []
                for k in range(2):
                    target = targets[pl.ds(k * rows + row, 1), :]
                    hits.append((slots + start == target).astype(jnp.float32).astype(jnp.bfloat16))
                total = lax.dot_general(
                    left, jnp.concatenate(hits, axis=1), (((1,), (1,)), ((), ())),
                    preferred_element_type=jnp.float32)
                total = total[:fpad] + total[fpad:2 * fpad] + total[2 * fpad:]
                for i in range(span // width):
                    wide[start // width + i, pl.ds(pl.multiple_of(row * fpad, fpad), fpad), :] = (
                        total[:, i * width:(i + 1) * width])
            return 0

        lax.fori_loop(0, rows, one_row, 0, unroll=2)

        for m in range(count):
            for v in range(nvars):
                bs[m, v] = wide[m, pl.ds(v, rows, stride=fpad), :]
        for m in range(count):
            for v in range(nvars):
                total = -wide[m, pl.ds(nvars + v, rows, stride=fpad), :]
                for k in range(1, count):
                    total = total + (half_step * once[k]) * bs[(m - k) % count, v]
                bs[m, nvars + v] = total

    row_index = lax.broadcasted_iota(jnp.int32, (rows, width), 0)
    first_row, last_row = row_index == 0, row_index == rows - 1

    def operator(s, field, halo):
        a = cross[0, row_at(s), :]
        b = cross[1, row_at(s), :]
        nu = viscosity[row_at(s), :]
        ap, am = jnp.maximum(a, 0.0), jnp.minimum(a, 0.0)
        bp, bm = jnp.maximum(b, 0.0), jnp.minimum(b, 0.0)
        centre = axp[row_at(s, 1), :] + (ap - am) + (bp - bm) + 6.0 * nu
        s_low = axp[row_at(s), :] + nu
        r_low, r_high, t_low, t_high = ap + nu, nu - am, bp + nu, nu - bm
        here = [field[v, row_at(s, 1), :] for v in range(nvars)]
        results = []
        for v in range(nvars):
            value = here[v]
            below = jnp.where(first_row, halo[0, s, v:v + 1, :], pltpu.roll(value, 1, 0))
            above = jnp.where(last_row, halo[1, s, v:v + 1, :], pltpu.roll(value, rows - 1, 0))
            total = centre * value
            total = total - s_low * field[v, row_at(s), :] - nu * field[v, row_at(s, 2), :]
            total = total - r_low * below - r_high * above
            total = total - t_low * pltpu.roll(value, 1, 1) - t_high * pltpu.roll(value, width - 1, 1)
            for w in range(nvars):
                total = total + coupling[v, w] * here[w]
            results.append(total)
        return here, results

    for copy in local_copies(4):
        copy.wait()
    pl.when(has_zlo)(lambda: uz_copy(1).wait_recv())
    pl.when(has_zhi)(lambda: uz_copy(0).wait_recv())
    pl.when(jnp.logical_not(no_axial))(lambda: a_copy().wait_recv())
    pl.when(has_rlo)(lambda: ur_copy(1).wait_recv())
    pl.when(has_rhi)(lambda: ur_copy(0).wait_recv())

    def prepare(start, stop):
        @pl.loop(start, stop)
        def _(s):
            here, results = operator(s, up, ur)
            for v in range(nvars):
                f[v, row_at(s, 1), :] = here[v] - half_step * results[v]

    prepare(planes - 1, planes)

    def gather(first):
        return [sum((br[n, v] for n in range(1, count)), br[0, v]) for v in range(first, first + nvars)]

    pairs = [(once[k], once[k] - half_step * twice[k]) for k in range(count)]
    zero_step = lax.convert_element_type(core, jnp.int32) == 0
    terms = []
    for d in range(1, chips):
        terms.append((xb, d - 1, pairs[2 * d]))
    for d in range(chips):
        low, high = pairs[(2 * d - 1) % count], pairs[(2 * d + 1) % count]
        terms.append((cb, d, tuple(jnp.where(zero_step, jnp.float32(lo), jnp.float32(hi)) for lo, hi in zip(low, high))))

    def process(j):
        s0, n = chunks[j]
        for d in range(chips):
            c_copy(d, j).wait_recv()
        if s0 == 0:
            @pl.when(stator)
            def _():
                for n in range(count):
                    face_copy(0, n).wait_recv()
                for v, inflow in enumerate(gather(0)):
                    f[v, rows_of(0, 1, 1), :] += half_step * inflow

        for s in range(s0, s0 + n):
            for v in range(nvars):
                own = up[v, rows_of(s, 1, 1), :]
                spectral = pairs[0][0] * own if pairs[0][0] else None
                combined = pairs[0][1] * own
                for buffer, slot, (c, g) in terms:
                    value = buffer[slot, v, rows_of(s), :]
                    spectral = c * value if spectral is None else spectral + c * value
                    combined = combined + g * value
                new = f[v, rows_of(s, 1, 1), :] - pseudo_step * spectral
                f[v, rows_of(s, 1, 1), :] = new
                out[v, rows_of(s), :] = combined
                frs[0, s, v:v + 1, :] = new[rows - 1:rows]
                frs[1, s, v:v + 1, :] = new[0:1]
                if s == planes - 1:
                    wv[pl.ds(nvars + v, rows, stride=fpad), :] = axp[rows_of(planes), :] * (new + half_step * spectral)
        pl.when(has_rhi)(lambda: fr_copy(1, j).start())
        pl.when(has_rlo)(lambda: fr_copy(0, j).start())
        if s0 == planes - 1:
            pl.when(has_zhi)(lambda: fz_copy(1).start())

            @pl.when(face)
            def _():
                speed = axp[rows_of(planes), :]
                for v in range(nvars):
                    wv[pl.ds(v, rows, stride=fpad), :] = speed * up[v, rows_of(planes), :]
                scatter()
                for m in range(count):
                    face_copy(m, me).start()
        if s0 == 0:
            pl.when(has_zlo)(lambda: fz_copy(0).start())

    def finish(s, n):
        @pl.loop(s, s + n)
        def _(s):
            _, results = operator(s, f, fr)
            for v in range(nvars):
                out[v, row_at(s), :] += results[v]

    done = {0, planes - 1}
    ready = set()

    def finals(j):
        s0, n = chunks[j]
        pl.when(has_rlo)(lambda: fr_copy(1, j).wait_recv())
        pl.when(has_rhi)(lambda: fr_copy(0, j).wait_recv())
        ready.update(range(s0, s0 + n))
        able = [s for s in range(1, planes - 1)
                if s not in done and {s - 1, s, s + 1} <= ready]
        if able:
            done.update(able)
            finish(able[0], len(able))
        if j == len(chunks) - 2:
            pl.when(has_zlo)(lambda: fz_copy(1).wait_recv())
            finish(0, 1)
        if j == len(chunks) - 1:
            pl.when(has_zhi)(lambda: fz_copy(0).wait_recv())
            finish(planes - 1, 1)

            @pl.when(stator)
            def _():
                for v, inflow in enumerate(gather(nvars)):
                    out[v, rows_of(0), :] += inflow

    steps = len(chunks)
    for j in range(steps + 2):
        if j < steps:
            for d in range(1, chips):
                x_copy(d, j).wait_recv()
                c_copy(d, j).start()
        if 1 <= j <= steps:
            process(j - 1)
        if j == 1:
            for later in range(early, steps):
                for d in range(1, chips):
                    x_copy(d, later).start()
            prepare(0, planes - 1)
        if 2 <= j:
            finals(j - 2)

    for j in range(steps):
        for d in range(1, chips):
            x_copy(d, j).wait_send()
        for d in range(chips):
            c_copy(d, j).wait_send()
    @pl.when(has_rhi)
    def _():
        ur_copy(1).wait_send()
        for j in range(steps):
            fr_copy(1, j).wait_send()

    @pl.when(has_rlo)
    def _():
        ur_copy(0).wait_send()
        for j in range(steps):
            fr_copy(0, j).wait_send()

    @pl.when(has_zhi)
    def _():
        uz_copy(1).wait_send()
        fz_copy(1).wait_send()

    @pl.when(has_zlo)
    def _():
        uz_copy(0).wait_send()
        fz_copy(0).wait_send()

    pl.when(sends_axial)(lambda: a_copy().wait_send())

    @pl.when(face)
    def _():
        for m in range(count):
            face_copy(m, me).wait_send()


def body(state, axial_speed, cross_speed, viscosity, coupling, targets, shares):
    count, streams, rads = (lax.axis_size(name) for name in ("inst", "stream", "rad"))
    _, nvars, planes, rows, width = state.shape
    chips, chunks = count // 2, len(chunk_list(planes))
    vpad, fpad = -(-nvars // 8) * 8, -(-2 * nvars // 16) * 16
    cells = planes * rows
    vmem = pl.BlockSpec(memory_space=pltpu.VMEM)
    hbm = pl.BlockSpec(memory_space=pltpu.HBM)
    dma = pltpu.SemaphoreType.DMA
    buf = lambda *shape: pltpu.VMEM(shape, jnp.float32)
    result = pl.pallas_call(
        functools.partial(kernel, count, streams, rads, nvars, planes, rows, width),
        out_shape=jax.ShapeDtypeStruct((nvars, cells, width), jnp.float32),
        in_specs=[hbm, hbm, hbm, hbm, pl.BlockSpec(memory_space=pltpu.SMEM), hbm, hbm],
        out_specs=vmem,
        scratch_shapes=[
            buf(nvars, cells + 2 * rows, width), buf(cells + rows, width),
            buf(2, cells, width), buf(cells, width),
            pltpu.VMEM((2 * rows, width), jnp.int32), buf(rows, width),
            buf(count, rows * fpad, width),
            buf(chips - 1, nvars, cells, width), buf(chips, nvars, cells, width),
            buf(nvars, cells + 2 * rows, width),
            buf(2, planes, vpad, width), buf(2, planes, vpad, width),
            buf(2, planes, vpad, width), buf(2, planes, vpad, width),
            buf(rows * fpad, width),
            buf(count, 2 * nvars, rows, width), buf(count, 2 * nvars, rows, width),
            dma((6,)), dma((chips - 1, chunks)), dma((chips - 1, chunks)),
            dma((chips, chunks)), dma((chips, chunks)),
            dma((2,)), dma((2,)), dma((2,)), dma((2,)), dma((1,)), dma((1,)),
            dma((2,)), dma((2,)), dma((2, chunks)), dma((2, chunks)),
            dma((count,)), dma((count,)),
        ],
        compiler_params=pltpu.CompilerParams(
            collective_id=0, has_side_effects=True, vmem_limit_bytes=63 * 1024 * 1024),
    )(
        state.reshape(nvars, cells, width), axial_speed.reshape(cells, width),
        cross_speed.reshape(2, cells, width), viscosity.reshape(cells, width), coupling,
        jnp.transpose(targets[0], (2, 0, 1)).reshape(2 * rows, width), shares[0],
    )
    return state - pseudo_step * result.reshape(state.shape)


def solution(mesh):
    in_specs = (
        P("inst", None, "stream", "rad", None),
        P("stream", "rad", None),
        P(None, "stream", "rad", None),
        P("stream", "rad", None),
        P(),
        P("inst", "rad", None, None),
        P("inst", "rad", None),
    )
    out_specs = P("inst", None, "stream", "rad", None)
    return jax.shard_map(body, mesh=mesh, in_specs=in_specs, out_specs=out_specs, check_vma=False)
```

```python
import functools
import math

import jax
import jax.numpy as jnp
from jax import lax
from jax.experimental import pallas as pl
from jax.experimental.pallas import tpu as pltpu
from jax.sharding import PartitionSpec as P

omega_scale = 0.5
pseudo_step = 0.5
MESH = pl.DeviceIdType.MESH


def coefficients(count):
    once = [0.0] + [
        omega_scale * 0.5 * (-1.0) ** k * math.cos(math.pi * k / count) / math.sin(math.pi * k / count)
        for k in range(1, count)
    ]
    twice = [sum(once[i] * once[(k - i) % count] for i in range(count)) for k in range(count)]
    return once, twice


def chunk_list(planes):
    chunks = [(planes - 1, 1)]
    start = 1
    while start < planes - 1:
        size = min(2, planes - 1 - start)
        chunks.append((start, size))
        start += size
    chunks.insert(len(chunks) - 2, (0, 1))
    return chunks


def kernel(
    count, streams, rads, nvars, planes, rows, width,
    u, axial, cross_in, viscosity_in, coupling, targets_in, shares_in, out,
    up, axp, cross, viscosity, targets, shares, wide, xb, cb, f, ur, urs, fr, frs, wv, bs, bp, br,
    local_sem, x_send, x_recv, c_send, c_recv, uz_send, uz_recv, fz_send, fz_recv,
    a_send, a_recv, ur_send, ur_recv, fr_send, fr_recv, b_send, b_recv, p_send, p_recv,
):
    chips = count // 2
    chunks = chunk_list(planes)
    once, twice = coefficients(count)
    half_step = 0.5 * pseudo_step
    vpad = fr.shape[2]
    me = lax.axis_index("inst")
    z = lax.axis_index("stream")
    r = lax.axis_index("rad")
    chip, core = me // 2, lax.rem(me, 2)
    peer = me + 1 - 2 * core
    has_zlo, has_zhi = z > 0, z < streams - 1
    has_rlo, has_rhi = r > 0, r < rads - 1
    face = z == streams // 2 - 1
    stator = z == streams // 2

    def rows_of(s, n=1, shift=0):
        return pl.ds((s + shift) * rows, n * rows)

    def row_at(s, shift=0):
        return pl.ds(pl.multiple_of((s + shift) * rows, rows), rows)

    def x_copy(d, j):
        s, n = chunks[j]
        return pltpu.make_async_remote_copy(
            src_ref=u.at[:, rows_of(s, n), :], dst_ref=xb.at[d - 1, :, rows_of(s, n), :],
            send_sem=x_send.at[d - 1, j], recv_sem=x_recv.at[d - 1, j],
            device_id={"inst": lax.rem(chip + d, chips) * 2 + core}, device_id_type=MESH)

    def c_copy(d, j):
        s, n = chunks[j]
        source = u if d == 0 else xb.at[d - 1]
        return pltpu.make_async_remote_copy(
            src_ref=source.at[:, rows_of(s, n), :], dst_ref=cb.at[d, :, rows_of(s, n), :],
            send_sem=c_send.at[d, j], recv_sem=c_recv.at[d, j],
            device_id={"inst": peer}, device_id_type=MESH)

    def z_copy(to_high, source, shift, field, send, recv):
        own = rows_of(planes - 1 if to_high else 0, 1, shift)
        landing = rows_of(0 if to_high else planes + 1)
        return pltpu.make_async_remote_copy(
            src_ref=source.at[:, own, :], dst_ref=field.at[:, landing, :],
            send_sem=send.at[1 - to_high], recv_sem=recv.at[1 - to_high],
            device_id={"stream": z + 1 if to_high else z - 1}, device_id_type=MESH)

    def uz_copy(to_high):
        return z_copy(to_high, u, 0, up, uz_send, uz_recv)

    def fz_copy(to_high):
        return z_copy(to_high, f, 1, f, fz_send, fz_recv)

    def a_copy():
        return pltpu.make_async_remote_copy(
            src_ref=axial.at[rows_of(planes - 1), :], dst_ref=axp.at[rows_of(0), :],
            send_sem=a_send.at[0], recv_sem=a_recv.at[0],
            device_id={"stream": z + 1}, device_id_type=MESH)

    def ur_copy(to_high):
        side = 1 - to_high
        return pltpu.make_async_remote_copy(
            src_ref=urs.at[side], dst_ref=ur.at[side],
            send_sem=ur_send.at[side], recv_sem=ur_recv.at[side],
            device_id={"rad": r + 1 if to_high else r - 1}, device_id_type=MESH)

    def fr_copy(to_high, j):
        s, n = chunks[j]
        side = 1 - to_high
        return pltpu.make_async_remote_copy(
            src_ref=frs.at[side, pl.ds(s, n)], dst_ref=fr.at[side, pl.ds(s, n)],
            send_sem=fr_send.at[side, j], recv_sem=fr_recv.at[side, j],
            device_id={"rad": r + 1 if to_high else r - 1}, device_id_type=MESH)

    def pair_copy(q):
        return pltpu.make_async_remote_copy(
            src_ref=bs.at[2 * q + 1 - core], dst_ref=bp.at[q],
            send_sem=p_send.at[q], recv_sem=p_recv.at[q],
            device_id={"inst": peer}, device_id_type=MESH)

    def face_copy(q, slot):
        return pltpu.make_async_remote_copy(
            src_ref=bs.at[2 * q + core], dst_ref=br.at[slot],
            send_sem=b_send.at[q], recv_sem=b_recv.at[slot],
            device_id={"inst": 2 * q + core, "stream": z + 1}, device_id_type=MESH)

    def local_copies(first=0, last=6):
        pairs = [
            (u, up.at[:, rows_of(0, planes, 1), :]),
            (axial, axp.at[rows_of(0, planes, 1), :]),
            (targets_in, targets),
            (shares_in, shares),
            (viscosity_in, viscosity),
            (cross_in, cross),
        ]
        return [pltpu.make_async_copy(*pairs[i], local_sem.at[i]) for i in range(first, last)]

    for copy in local_copies():
        copy.start()

    barrier = pltpu.get_barrier_semaphore()

    def greet(**device):
        pl.semaphore_signal(barrier, inc=1, device_id=device, device_id_type=MESH)

    greet(inst=peer)
    for d in range(1, chips):
        greet(inst=lax.rem(chip + d, chips) * 2 + core)
    pl.when(has_zlo)(lambda: greet(stream=z - 1))
    pl.when(has_zhi)(lambda: greet(stream=z + 1))
    pl.when(has_rlo)(lambda: greet(rad=r - 1))
    pl.when(has_rhi)(lambda: greet(rad=r + 1))
    for d in range(1, count):
        other = lax.rem(me + d, count)
        pl.when(face)(functools.partial(greet, inst=other, stream=z + 1))
        pl.when(stator)(functools.partial(greet, inst=other, stream=z - 1))
    one = lambda flag: flag.astype(jnp.int32)
    expected = chips + one(has_zlo) + one(has_zhi) + one(has_rlo) + one(has_rhi)
    expected = expected + (count - 1) * (one(face) + one(stator))

    plane_zero = jnp.zeros((rows, width), jnp.float32)

    def zero_plane(field, p):
        for v in range(nvars):
            field[v, rows_of(p), :] = plane_zero

    @pl.when(jnp.logical_not(has_zlo))
    def _():
        zero_plane(up, 0)
        zero_plane(f, 0)

    @pl.when(jnp.logical_not(has_zhi))
    def _():
        zero_plane(up, planes + 1)
        zero_plane(f, planes + 1)

    no_axial = jnp.logical_or(jnp.logical_not(has_zlo), stator)

    @pl.when(no_axial)
    def _():
        axp[rows_of(0), :] = plane_zero

    @pl.when(jnp.logical_not(has_rlo))
    def _():
        ur[0] = jnp.zeros(ur.shape[1:], jnp.float32)
        fr[0] = jnp.zeros(fr.shape[1:], jnp.float32)

    @pl.when(jnp.logical_not(has_rhi))
    def _():
        ur[1] = jnp.zeros(ur.shape[1:], jnp.float32)
        fr[1] = jnp.zeros(fr.shape[1:], jnp.float32)

    urs[...] = jnp.zeros(urs.shape, jnp.float32)
    frs[...] = jnp.zeros(frs.shape, jnp.float32)
    wv[...] = jnp.zeros(wv.shape, jnp.float32)

    pl.semaphore_wait(barrier, expected)

    early = min(5, len(chunks))
    for j in range(early):
        for d in range(1, chips):
            x_copy(d, j).start()
    for j in range(len(chunks)):
        c_copy(0, j).start()
    pl.when(has_zhi)(lambda: uz_copy(1).start())
    pl.when(has_zlo)(lambda: uz_copy(0).start())
    sends_axial = jnp.logical_and(has_zhi, jnp.logical_not(face))
    pl.when(sends_axial)(lambda: a_copy().start())

    for copy in local_copies(0, 4):
        copy.wait()

    @pl.loop(0, planes)
    def _(s):
        base = (s + 1) * rows
        for v in range(nvars):
            urs[0, s, v:v + 1, :] = up[v, pl.ds(base + rows - 1, 1), :]
            urs[1, s, v:v + 1, :] = up[v, pl.ds(base, 1), :]

    pl.when(has_rhi)(lambda: ur_copy(1).start())
    pl.when(has_rlo)(lambda: ur_copy(0).start())

    fpad = wv.shape[0] // rows

    def scatter():
        span = min(count, 4) * width

        def one_row(row, _):
            flux = wv[pl.ds(pl.multiple_of(row * fpad, fpad), fpad), :]
            share = shares[pl.ds(row, 1), :]
            parts = []
            for value in (flux * share, flux * (1.0 - share)):
                high = value.astype(jnp.bfloat16).astype(jnp.float32)
                rest = value - high
                middle = rest.astype(jnp.bfloat16).astype(jnp.float32)
                stack = jnp.concatenate([high, middle, rest - middle], axis=0)
                parts.append(stack.astype(jnp.bfloat16))
            left = jnp.concatenate(parts, axis=1)
            slots = lax.broadcasted_iota(jnp.int32, (span, width), 0)
            for start in range(0, count * width, span):
                hits = []
                for k in range(2):
                    target = targets[pl.ds(k * rows + row, 1), :]
                    hits.append((slots + start == target).astype(jnp.float32).astype(jnp.bfloat16))
                total = lax.dot_general(
                    left, jnp.concatenate(hits, axis=1), (((1,), (1,)), ((), ())),
                    preferred_element_type=jnp.float32)
                total = total[:fpad] + total[fpad:2 * fpad] + total[2 * fpad:]
                for i in range(span // width):
                    wide[start // width + i, pl.ds(pl.multiple_of(row * fpad, fpad), fpad), :] = (
                        total[:, i * width:(i + 1) * width])
            return 0

        lax.fori_loop(0, rows, one_row, 0, unroll=2)

        for m in range(count):
            for v in range(nvars):
                bs[m, v] = wide[m, pl.ds(v, rows, stride=fpad), :]
        for m in range(count):
            for v in range(nvars):
                total = -wide[m, pl.ds(nvars + v, rows, stride=fpad), :]
                for k in range(1, count):
                    total = total + (half_step * once[k]) * bs[(m - k) % count, v]
                bs[m, nvars + v] = total

    row_index = lax.broadcasted_iota(jnp.int32, (rows, width), 0)
    first_row, last_row = row_index == 0, row_index == rows - 1

    def operator(s, field, halo):
        a = cross[0, row_at(s), :]
        b = cross[1, row_at(s), :]
        nu = viscosity[row_at(s), :]
        ap, am = jnp.maximum(a, 0.0), jnp.minimum(a, 0.0)
        bp, bm = jnp.maximum(b, 0.0), jnp.minimum(b, 0.0)
        centre = axp[row_at(s, 1), :] + (ap - am) + (bp - bm) + 6.0 * nu
        s_low = axp[row_at(s), :] + nu
        r_low, r_high, t_low, t_high = ap + nu, nu - am, bp + nu, nu - bm
        here = [field[v, row_at(s, 1), :] for v in range(nvars)]
        results = []
        for v in range(nvars):
            value = here[v]
            below = jnp.where(first_row, halo[0, s, v:v + 1, :], pltpu.roll(value, 1, 0))
            above = jnp.where(last_row, halo[1, s, v:v + 1, :], pltpu.roll(value, rows - 1, 0))
            total = centre * value
            total = total - s_low * field[v, row_at(s), :] - nu * field[v, row_at(s, 2), :]
            total = total - r_low * below - r_high * above
            total = total - t_low * pltpu.roll(value, 1, 1) - t_high * pltpu.roll(value, width - 1, 1)
            for w in range(nvars):
                total = total + coupling[v, w] * here[w]
            results.append(total)
        return here, results

    for copy in local_copies(4):
        copy.wait()
    pl.when(has_zlo)(lambda: uz_copy(1).wait_recv())
    pl.when(has_zhi)(lambda: uz_copy(0).wait_recv())
    pl.when(jnp.logical_not(no_axial))(lambda: a_copy().wait_recv())
    pl.when(has_rlo)(lambda: ur_copy(1).wait_recv())
    pl.when(has_rhi)(lambda: ur_copy(0).wait_recv())

    def prepare(start, stop):
        @pl.loop(start, stop)
        def _(s):
            here, results = operator(s, up, ur)
            for v in range(nvars):
                f[v, row_at(s, 1), :] = here[v] - half_step * results[v]

    prepare(planes - 1, planes)

    def gather(first):
        return [sum((br[n, v] for n in range(1, chips)), br[0, v]) for v in range(first, first + nvars)]

    pairs = [(once[k], once[k] - half_step * twice[k]) for k in range(count)]
    zero_step = lax.convert_element_type(core, jnp.int32) == 0
    terms = []
    for d in range(1, chips):
        terms.append((xb, d - 1, pairs[2 * d]))
    for d in range(chips):
        low, high = pairs[(2 * d - 1) % count], pairs[(2 * d + 1) % count]
        terms.append((cb, d, tuple(jnp.where(zero_step, jnp.float32(lo), jnp.float32(hi)) for lo, hi in zip(low, high))))

    def process(j):
        s0, n = chunks[j]
        for d in range(chips):
            c_copy(d, j).wait_recv()
        if s0 == 0:
            @pl.when(stator)
            def _():
                for n in range(chips):
                    face_copy(0, n).wait_recv()
                for v, inflow in enumerate(gather(0)):
                    f[v, rows_of(0, 1, 1), :] += half_step * inflow

        for s in range(s0, s0 + n):
            for v in range(nvars):
                own = up[v, rows_of(s, 1, 1), :]
                spectral = pairs[0][0] * own if pairs[0][0] else None
                combined = pairs[0][1] * own
                for buffer, slot, (c, g) in terms:
                    value = buffer[slot, v, rows_of(s), :]
                    spectral = c * value if spectral is None else spectral + c * value
                    combined = combined + g * value
                new = f[v, rows_of(s, 1, 1), :] - pseudo_step * spectral
                f[v, rows_of(s, 1, 1), :] = new
                out[v, rows_of(s), :] = pseudo_step * combined
                frs[0, s, v:v + 1, :] = new[rows - 1:rows]
                frs[1, s, v:v + 1, :] = new[0:1]
                if s == planes - 1:
                    wv[pl.ds(nvars + v, rows, stride=fpad), :] = axp[rows_of(planes), :] * (new + half_step * spectral)
        pl.when(has_rhi)(lambda: fr_copy(1, j).start())
        pl.when(has_rlo)(lambda: fr_copy(0, j).start())
        if s0 == planes - 1:
            pl.when(has_zhi)(lambda: fz_copy(1).start())

            @pl.when(face)
            def _():
                speed = axp[rows_of(planes), :]
                for v in range(nvars):
                    wv[pl.ds(v, rows, stride=fpad), :] = speed * up[v, rows_of(planes), :]
                scatter()
                for q in range(chips):
                    pair_copy(q).start()
                for q in range(chips):
                    pair_copy(q).wait_recv()
                    slot = 2 * q + core
                    for v in range(2 * nvars):
                        bs[slot, v] = bs[slot, v] + bp[q, v]
                    face_copy(q, chip).start()
        if s0 == 0:
            pl.when(has_zlo)(lambda: fz_copy(0).start())

    def finish(s, n):
        @pl.loop(s, s + n)
        def _(s):
            _, results = operator(s, f, fr)
            for v in range(nvars):
                out[v, row_at(s), :] += pseudo_step * results[v]

    done = {0, planes - 1}
    ready = set()

    def finals(j):
        s0, n = chunks[j]
        pl.when(has_rlo)(lambda: fr_copy(1, j).wait_recv())
        pl.when(has_rhi)(lambda: fr_copy(0, j).wait_recv())
        ready.update(range(s0, s0 + n))
        able = [s for s in range(1, planes - 1)
                if s not in done and {s - 1, s, s + 1} <= ready]
        if able:
            done.update(able)
            finish(able[0], len(able))
        if j == len(chunks) - 2:
            pl.when(has_zlo)(lambda: fz_copy(1).wait_recv())
            finish(0, 1)
        if j == len(chunks) - 1:
            pl.when(has_zhi)(lambda: fz_copy(0).wait_recv())
            finish(planes - 1, 1)

            @pl.when(stator)
            def _():
                for v, inflow in enumerate(gather(nvars)):
                    out[v, rows_of(0), :] += pseudo_step * inflow

    steps = len(chunks)
    for j in range(steps + 2):
        if j < steps:
            for d in range(1, chips):
                x_copy(d, j).wait_recv()
                c_copy(d, j).start()
        if 1 <= j <= steps:
            process(j - 1)
        if j == 1:
            for later in range(early, steps):
                for d in range(1, chips):
                    x_copy(d, later).start()
            prepare(0, planes - 1)
        if 2 <= j:
            finals(j - 2)

    for j in range(steps):
        for d in range(1, chips):
            x_copy(d, j).wait_send()
        for d in range(chips):
            c_copy(d, j).wait_send()
    @pl.when(has_rhi)
    def _():
        ur_copy(1).wait_send()
        for j in range(steps):
            fr_copy(1, j).wait_send()

    @pl.when(has_rlo)
    def _():
        ur_copy(0).wait_send()
        for j in range(steps):
            fr_copy(0, j).wait_send()

    @pl.when(has_zhi)
    def _():
        uz_copy(1).wait_send()
        fz_copy(1).wait_send()

    @pl.when(has_zlo)
    def _():
        uz_copy(0).wait_send()
        fz_copy(0).wait_send()

    pl.when(sends_axial)(lambda: a_copy().wait_send())

    @pl.when(face)
    def _():
        for q in range(chips):
            pair_copy(q).wait_send()
            face_copy(q, chip).wait_send()


def body(state, axial_speed, cross_speed, viscosity, coupling, targets, shares):
    count, streams, rads = (lax.axis_size(name) for name in ("inst", "stream", "rad"))
    _, nvars, planes, rows, width = state.shape
    chips, chunks = count // 2, len(chunk_list(planes))
    vpad, fpad = -(-nvars // 8) * 8, -(-2 * nvars // 16) * 16
    cells = planes * rows
    vmem = pl.BlockSpec(memory_space=pltpu.VMEM)
    hbm = pl.BlockSpec(memory_space=pltpu.HBM)
    dma = pltpu.SemaphoreType.DMA
    buf = lambda *shape: pltpu.VMEM(shape, jnp.float32)
    result = pl.pallas_call(
        functools.partial(kernel, count, streams, rads, nvars, planes, rows, width),
        out_shape=jax.ShapeDtypeStruct((nvars, cells, width), jnp.float32),
        in_specs=[hbm, hbm, hbm, hbm, pl.BlockSpec(memory_space=pltpu.SMEM), hbm, hbm],
        out_specs=vmem,
        scratch_shapes=[
            buf(nvars, cells + 2 * rows, width), buf(cells + rows, width),
            buf(2, cells, width), buf(cells, width),
            pltpu.VMEM((2 * rows, width), jnp.int32), buf(rows, width),
            buf(count, rows * fpad, width),
            buf(chips - 1, nvars, cells, width), buf(chips, nvars, cells, width),
            buf(nvars, cells + 2 * rows, width),
            buf(2, planes, vpad, width), buf(2, planes, vpad, width),
            buf(2, planes, vpad, width), buf(2, planes, vpad, width),
            buf(rows * fpad, width),
            buf(count, 2 * nvars, rows, width), buf(chips, 2 * nvars, rows, width), buf(chips, 2 * nvars, rows, width),
            dma((6,)), dma((chips - 1, chunks)), dma((chips - 1, chunks)),
            dma((chips, chunks)), dma((chips, chunks)),
            dma((2,)), dma((2,)), dma((2,)), dma((2,)), dma((1,)), dma((1,)),
            dma((2,)), dma((2,)), dma((2, chunks)), dma((2, chunks)),
            dma((chips,)), dma((chips,)), dma((chips,)), dma((chips,)),
        ],
        compiler_params=pltpu.CompilerParams(
            collective_id=0, has_side_effects=True, vmem_limit_bytes=63 * 1024 * 1024),
    )(
        state.reshape(nvars, cells, width), axial_speed.reshape(cells, width),
        cross_speed.reshape(2, cells, width), viscosity.reshape(cells, width), coupling,
        jnp.transpose(targets[0], (2, 0, 1)).reshape(2 * rows, width), shares[0],
    )
    return state - result.reshape(state.shape)


def solution(mesh):
    in_specs = (
        P("inst", None, "stream", "rad", None),
        P("stream", "rad", None),
        P(None, "stream", "rad", None),
        P("stream", "rad", None),
        P(),
        P("inst", "rad", None, None),
        P("inst", "rad", None),
    )
    out_specs = P("inst", None, "stream", "rad", None)
    return jax.shard_map(body, mesh=mesh, in_specs=in_specs, out_specs=out_specs, check_vma=False)
```
